1024 devices in a mesh: row: 32 (over z_hi, x, y), col: 32 (over z_lo, core).
Axes of the slice: x: 4, y: 4, z: 32 (z_hi: 2, z_lo: 16; z = z_hi * 16 + z_lo), core: 2. Of those that a mesh axis runs over, the one named last changes fastest.
Arguments:
- p_blocks: bfloat16 [32, 32, 3, 128, 128], P('row', 'col'), may hold values from -1.5 to 1.5
- p_rows: int32 [32, 32, 3], P('row', 'col'), may hold values from 0 to 12, as said below
- p_cols: int32 [32, 32, 3], P('row', 'col'), may hold values from 0 to 12
- p_count: int32 [32, 32], P('row', 'col'), may hold values from 2 to 3, as said below
- kept_rows: int32 [32, 32, 6], P('row', 'col'), may hold values from 0 to 12, as said below
- kept_cols: int32 [32, 32, 6], P('row', 'col'), may hold values from 0 to 12
Outputs:
- square_blocks: float32 [32, 32, 6, 128, 128], P('row', 'col')
The draws below stay inside these ranges and needn't reach their ends.
Inputs may be any that keep to these rules, and one draw needn't show every extreme that they name: `p_rows`: within one device tile the used slots name distinct blocks. `p_count`: some device tile uses all 3 slots. `kept_rows`: within one device tile the kept blocks are distinct.
All inputs are finite; a program needn't handle non-finite values.
Results may differ from the reference program's by a relative error of at most 0.0003.
Values may be sent and summed in bfloat16 or wider, within the bound.
A program may use at most 32 MiB of HBM per device.

```python
import jax
import jax.numpy as jnp
from jax import lax

BS = 128
TBC = 13
SLOTS = 3
OUT_SLOTS = 6
TBR = 13
NB = 416
N_ROW = 32
N_COL = 32


def pattern(key):
    key_perm, key_count = jax.random.split(jax.random.fold_in(key, 101))
    cells = TBR * TBC
    tiles = N_ROW * N_COL
    perm_keys = jax.random.split(key_perm, tiles)
    chosen = jax.vmap(lambda one_key: jax.random.permutation(one_key, cells))(perm_keys)[:, :SLOTS]
    counts = jax.random.randint(key_count, (tiles,), 2, SLOTS + 1)
    special = jax.random.randint(jax.random.fold_in(key_count, 7), (), 0, tiles)
    counts = jnp.where(jnp.arange(tiles) == special, SLOTS, counts)
    rows = (chosen // TBC).reshape(N_ROW, N_COL, SLOTS).astype(jnp.int32)
    cols = (chosen % TBC).reshape(N_ROW, N_COL, SLOTS).astype(jnp.int32)
    return (rows, cols, counts.reshape(N_ROW, N_COL).astype(jnp.int32))


def kept_pattern(key):
    rows, cols, counts = pattern(key)
    cells = TBR * TBC
    tiles = N_ROW * N_COL
    is_valid = (jnp.arange(SLOTS)[None, None, :] < counts[:, :, None]).astype(jnp.int32)
    global_rows = jnp.arange(N_ROW)[:, None, None] * TBR + rows
    global_cols = jnp.arange(N_COL)[None, :, None] * TBC + cols
    occupied = jnp.zeros((NB, NB), jnp.int32).at[global_rows.reshape(-1), global_cols.reshape(-1)].add(is_valid.reshape(-1))
    squared = jnp.dot(occupied, occupied, preferred_element_type=jnp.int32)
    per_tile = squared.reshape(N_ROW, TBR, N_COL, TBC).transpose(0, 2, 1, 3).reshape(tiles, cells)
    tie_keys = jax.random.split(jax.random.fold_in(key, 202), tiles)
    ties = jax.vmap(lambda one_key: jax.random.permutation(one_key, cells))(tie_keys)
    scores = per_tile * cells + ties
    unused, picked = jax.lax.top_k(scores, OUT_SLOTS)
    kept_r = (picked // TBC).reshape(N_ROW, N_COL, OUT_SLOTS).astype(jnp.int32)
    kept_c = (picked % TBC).reshape(N_ROW, N_COL, OUT_SLOTS).astype(jnp.int32)
    return (kept_r, kept_c)


def draw_p_rows(key, part):
    return pattern(key)[0]


def draw_p_cols(key, part):
    return pattern(key)[1]


def draw_p_count(key, part):
    return pattern(key)[2]


def draw_kept_rows(key, part):
    return kept_pattern(key)[0]


def draw_kept_cols(key, part):
    return kept_pattern(key)[1]


def shard_levels(own_key, extent, cuts, smallest, high):
    loudness = 1.0
    for dim, shards_of in cuts:
        steps = jax.random.uniform(jax.random.fold_in(jax.random.fold_in(own_key, 6), dim), (shards_of,), jnp.float32, smallest / len(cuts), high / len(cuts))
        loudness = loudness * jnp.repeat(jnp.exp(steps), extent[dim] // shards_of).reshape((-1,) + (1,) * (len(extent) - 1 - dim))
    return loudness


def bell_draw(rng, shape, width, limit, cuts=(), kind=jnp.bfloat16):
    level = shard_levels(rng, shape, cuts, -0.22, 0.18) if cuts else 1.0
    values = jax.random.normal(rng, shape, jnp.float32) * width * level
    return jnp.minimum(jnp.maximum(values, -limit), limit).astype(kind)


def setup_inputs(seed: int = 0) -> dict:
    splits = jax.random.split(jax.random.key(seed), 7)
    p_blocks = bell_draw(splits[0], (N_ROW, N_COL, SLOTS, BS, BS), 0.25, 1.5, ((0, 32), (1, 32)))
    p_rows = draw_p_rows(jax.random.fold_in(splits[6], 71), 0)
    p_cols = draw_p_cols(jax.random.fold_in(splits[6], 71), 0)
    p_count = draw_p_count(jax.random.fold_in(splits[6], 71), 0)
    kept_rows = draw_kept_rows(jax.random.fold_in(splits[6], 71), 0)
    kept_cols = draw_kept_cols(jax.random.fold_in(splits[6], 71), 0)
    return {"p_blocks": p_blocks, "p_rows": p_rows, "p_cols": p_cols, "p_count": p_count, "kept_rows": kept_rows, "kept_cols": kept_cols}


def reference(p_blocks, p_rows, p_cols, p_count, kept_rows, kept_cols):
    col_per_row = N_COL // N_ROW
    slot_ids = jnp.arange(SLOTS, dtype=jnp.int32)
    is_valid = (slot_ids[None, None, :] < p_count[:, :, None]).astype(jnp.float32)
    dense_blocks = p_blocks.astype(jnp.float32) * is_valid[:, :, :, None, None]

    def tile_rows(row_index):
        def one_tile(col_index, out_rows, out_cols):
            def inner_step(total, inner_piece):
                left_blocks = dense_blocks[row_index, inner_piece]
                left_rows = p_rows[row_index, inner_piece]
                left_cols = p_cols[row_index, inner_piece]
                group = inner_piece // col_per_row
                right_blocks = dense_blocks[group, col_index]
                right_rows = p_rows[group, col_index] - (inner_piece % col_per_row) * TBC
                right_cols = p_cols[group, col_index]
                weights = ((left_rows[None, :, None] == out_rows[:, None, None])
                           & (right_cols[None, None, :] == out_cols[:, None, None])
                           & (left_cols[None, :, None] == right_rows[None, None, :])).astype(jnp.float32)
                products = jnp.einsum('aik,bkj->abij', left_blocks, right_blocks, precision=lax.Precision.HIGHEST)
                total = total + jnp.einsum('oab,abij->oij', weights, products, precision=lax.Precision.HIGHEST)
                return total, None

            start = jnp.zeros((OUT_SLOTS, BS, BS), jnp.float32)
            total, unused = lax.scan(inner_step, start, jnp.arange(N_COL, dtype=jnp.int32))
            return total

        return jax.vmap(one_tile)(jnp.arange(N_COL, dtype=jnp.int32), kept_rows[row_index], kept_cols[row_index])

    return lax.map(tile_rows, jnp.arange(N_ROW, dtype=jnp.int32))
```

```python
import functools

import jax
import jax.numpy as jnp
from jax import lax
from jax.experimental import pallas as pl
from jax.experimental.pallas import tpu as pltpu
from jax.sharding import PartitionSpec as P

MESH = pl.DeviceIdType.MESH
BLOCK = 128
SLOTS = 3
KEPT = 6
META = SLOTS * BLOCK
TILE = META + 16
HALF = 208
HALVES = ((0, HALF), (HALF, TILE - HALF))
RUN = 16
NONE = 255


def device(z_hi, x, y, k, core):
    return (z_hi * 16 + x * 4 + y, k * 2 + core)


def turn(value, by):
    return lax.rem(value + by, 4)


def flag(condition):
    return jnp.where(condition, 1, 0)


def gather_kernel(
    p_rows, p_cols, p_count, blocks, row_tiles, col_tiles,
    meta, row_recv, col_recv, anti_recv, own_sem, send_own, send_row, send_pair, send_xy,
    ready_pair, ready_jump, ready_anti,
):
    row, col = lax.axis_index("row"), lax.axis_index("col")
    z_hi, x, y = row // 16, (row // 4) % 4, row % 4
    k, core = col // 2, col % 2
    here = functools.partial(device, z_hi, x, y)
    in_plane = lambda nx, ny: device(z_hi, nx, ny, k, core)
    pair = here(k, 1 - core)
    antipode = device(1 - z_hi, x, y, k, core)

    def signal(semaphore, target):
        pl.semaphore_signal(semaphore, inc=1, device_id=target, device_id_type=MESH)

    first_plane = (z_hi == 0) & (k == 0)
    is_late = first_plane & (x == 0) & (y == 0) & (core == 0)
    late_pair = first_plane & (x == 0) & (y == 0) & (core == 1)
    late_plane = first_plane & (core == 0) & ((x == 0) != (y == 0))

    copies = []

    def local(src, dst, number):
        copy = pltpu.make_async_copy(src, dst, own_sem.at[number])
        copy.start()
        copies.append(copy)

    mine_row, mine_col = row_tiles.at[col], col_tiles.at[row]
    local(blocks, mine_row.at[pl.ds(0, META)], 0)
    local(blocks, mine_col.at[pl.ds(0, META)], 1)

    barrier = pltpu.get_barrier_semaphore()

    @pl.when((core == 0) & (k > 0))
    def _():
        for other in range(2):
            signal(barrier, here(k - 1, other))

    @pl.when((core == 1) & (k < RUN - 1))
    def _():
        for other in range(2):
            signal(barrier, here(k + 1, other))

    @pl.when(jnp.logical_not(is_late))
    def _():
        signal(barrier, pair)
        for d in range(1, 4):
            signal(barrier, in_plane(turn(x, d), y))
            signal(barrier, in_plane(x, turn(y, d)))

    @pl.when(z_hi == 0)
    def _():
        signal(barrier, antipode)

    @pl.when((core == 1) & (k == 3))
    def _():
        for source in range(8, 16):
            for other in range(2):
                signal(barrier, here(source, other))

    @pl.when((core == 1) & (k == 7))
    def _():
        for source in range(12, 16):
            for other in range(2):
                signal(barrier, here(source, other))

    @pl.when(k < 8)
    def _():
        signal(barrier, here(12, 0))

    @pl.when(k < 4)
    def _():
        signal(barrier, here(8, 0))

    lane = lax.broadcasted_iota(jnp.int32, (16, BLOCK), 1)
    codes = jnp.zeros((16, BLOCK), jnp.int32)
    for slot in range(SLOTS):
        code = jnp.where(slot < p_count[0], p_rows[slot] * 16 + p_cols[slot], NONE)
        codes = jnp.where(lane == slot, code, codes)
    meta[...] = codes.astype(jnp.float32).astype(jnp.bfloat16)
    local(meta, mine_row.at[pl.ds(META, 16)], 2)
    local(meta, mine_col.at[pl.ds(META, 16)], 3)

    expected = (
        flag(k < RUN - 1) + flag(k > 0) + 1 - flag(late_pair) + 6 - flag(late_plane) + flag(k >= 8) + flag(k >= 12)
        + 8 * flag((core == 0) & (k == 8)) + 16 * flag((core == 0) & (k == 12)) + z_hi
    )
    pl.semaphore_wait(barrier, expected)

    @pl.when(z_hi == 1)
    def _():
        signal(ready_anti, antipode)

    @pl.when(is_late)
    def _():
        signal(ready_pair, pair)
        for d in range(1, 4):
            signal(ready_pair, in_plane(turn(x, d), y))
            signal(ready_pair, in_plane(x, turn(y, d)))

    @pl.when((core == 0) & (k == 8))
    def _():
        for source in range(0, 4):
            for other in range(2):
                signal(ready_jump, here(source, other))

    @pl.when((core == 0) & (k == 12))
    def _():
        for source in range(0, 8):
            for other in range(2):
                signal(ready_jump, here(source, other))

    for copy in copies:
        copy.wait()

    def send(src, dst, send_sem, recv_sem, target):
        return pltpu.make_async_remote_copy(
            src_ref=src, dst_ref=dst, send_sem=send_sem, recv_sem=recv_sem, device_id=target, device_id_type=MESH
        )

    def row_send(tile, send_sem, target):
        return send(row_tiles.at[tile], row_tiles.at[tile], send_sem, row_recv.at[tile], target)

    anti_send = send(mine_col, mine_col, send_own.at[0], anti_recv, antipode)
    left_send = row_send(col, send_own.at[1], here(k - 1, 1))
    right_send = row_send(col, send_own.at[2], here(k + 1, 0))
    pair_send = row_send(col, send_own.at[3], pair)
    jumps = (
        (k >= 12, row_send(col, send_own.at[4], here(7, 1))),
        (k >= 8, row_send(col, send_own.at[5], here(3, 1))),
        (k < 4, row_send(col, send_own.at[4], here(8, 0))),
        (k < 8, row_send(col, send_own.at[5], here(12, 0))),
    )

    @pl.when(z_hi == 1)
    def _():
        anti_send.start()

    for wanted, jump in jumps[:2]:
        pl.when(wanted)(jump.start)
    pl.when(k > 0)(left_send.start)
    pl.when(k < RUN - 1)(right_send.start)

    def half_send(side, tile, half, number, target):
        low, size = HALVES[half]
        part = col_tiles.at[tile, pl.ds(low, size)]
        return send(part, part, send_xy.at[side, number], col_recv.at[tile, half], target)

    def plane_tile(side, nx, ny):
        z = z_hi if side == 0 else 1 - z_hi
        return z * 16 + nx * 4 + ny

    def plane_own(side):
        mine = plane_tile(side, x, y)
        return [
            half_send(side, mine, half, number * 6 + (d - 1) * 2 + half, in_plane(turn(x, d), y) if along_x else in_plane(x, turn(y, d)))
            for number in range(2)
            for d in (2, 1, 3)
            for half in range(2)
            for along_x in ((half == 0) == (number == 0),)
        ]

    def plane_forward(side, d):
        from_x = plane_tile(side, turn(x, 4 - d), y)
        from_y = plane_tile(side, x, turn(y, 4 - d))
        first = [half_send(side, from_x, 0, 12 + (d - 1) * 6 + e - 1, in_plane(x, turn(y, e))) for e in (2, 1, 3)]
        second = [half_send(side, from_y, 1, 15 + (d - 1) * 6 + e - 1, in_plane(turn(x, e), y)) for e in (2, 1, 3)]
        return first, second

    def arrived(side, tile, half):
        half_send(side, tile, half, 0, pair).wait_recv()

    def plane_first(side):
        for copy in plane_own(side):
            copy.start()

    def plane_second(side):
        for d in (1, 3, 2):
            first, second = plane_forward(side, d)
            arrived(side, plane_tile(side, turn(x, 4 - d), y), 0)
            for copy in first:
                copy.start()
            arrived(side, plane_tile(side, x, turn(y, 4 - d)), 1)
            for copy in second:
                copy.start()

    def plane_rest(side):
        for d in range(1, 4):
            arrived(side, plane_tile(side, turn(x, d), y), 1)
            arrived(side, plane_tile(side, x, turn(y, d)), 0)
            for e in range(1, 4):
                for half in range(2):
                    arrived(side, plane_tile(side, turn(x, d), turn(y, e)), half)
        for copy in plane_own(side):
            copy.wait_send()
        for d in range(1, 4):
            for copies_of in plane_forward(side, d):
                for copy in copies_of:
                    copy.wait_send()

    @pl.when(late_plane)
    def _():
        pl.semaphore_wait(ready_pair, 1)

    plane_first(0)

    @pl.when(late_pair)
    def _():
        pl.semaphore_wait(ready_pair, 1)

    pair_send.start()
    plane_second(0)

    step = 2 * core - 1
    onward = here(jnp.clip(k - step, 0, RUN - 1), core)

    def is_valid(source):
        return (source >= 0) & (source < RUN)

    def goes_on(source):
        right = (k < RUN - 1) & jnp.logical_not((k == 7) & (source < 4)) & jnp.logical_not((k == 11) & (source < 8))
        left = (k > 0) & jnp.logical_not((k == 8) & (source >= 12)) & jnp.logical_not((k == 4) & (source >= 8))
        return jnp.where(core == 0, flag(right), flag(left)) == 1

    jump_at = 4
    anti_at = jnp.where((core == 1) & (z_hi == 0), jnp.where(k == 0, 8, 12), RUN)
    anti_next = RUN

    def anti_first():
        @pl.when(z_hi == 0)
        def _():
            pl.semaphore_wait(ready_anti, 1)
            anti_send.start()

        anti_send.wait_recv()
        plane_first(1)

    def jump_right():
        pl.semaphore_wait(ready_jump, flag(k < 8) + flag(k < 4))
        for wanted, jump in jumps[2:]:
            pl.when(wanted)(jump.start)

    def stream(t, carry):
        source = k + step * t

        @pl.when(is_valid(source))
        def _():
            for other in range(2):
                tile = source * 2 + other
                row_send(tile, send_row.at[tile], pair).wait_recv()
                pl.when(goes_on(source))(row_send(tile, send_row.at[tile], onward).start)
                row_send(tile, send_pair.at[tile], pair).start()

        @pl.when((t == jump_at) & (k < 8))
        def _():
            jump_right()

        @pl.when(t == anti_at)
        def _():
            anti_first()

        return carry

    lax.fori_loop(1, RUN, stream, 0)

    @pl.when(anti_at == RUN)
    def _():
        anti_first()

    plane_second(1)

    row_send(k * 2 + 1 - core, send_own.at[3], pair).wait_recv()

    def settle(t, carry):
        source, opposite = k + step * t, k - step * t

        @pl.when(is_valid(opposite))
        def _():
            for other in range(2):
                row_send(opposite * 2 + other, send_pair.at[0], pair).wait_recv()

        @pl.when(is_valid(source))
        def _():
            for other in range(2):
                tile = source * 2 + other
                pl.when(goes_on(source))(row_send(tile, send_row.at[tile], onward).wait_send)
                row_send(tile, send_pair.at[tile], pair).wait_send()

        return carry

    lax.fori_loop(1, RUN, settle, 0)
    plane_rest(0)
    plane_rest(1)
    anti_send.wait_send()
    pair_send.wait_send()
    pl.when(k > 0)(left_send.wait_send)
    pl.when(k < RUN - 1)(right_send.wait_send)
    for wanted, jump in jumps:
        pl.when(wanted)(jump.wait_send)


DEPTH = 8


def multiply_kernel(kept_rows, kept_cols, row_tiles, col_tiles, out, meta, codes, index, found, left, right, meta_sem, index_sem, sems):
    tiles = row_tiles.shape[0]
    loads = [
        pltpu.make_async_copy(tiles_of.at[:, pl.ds(META, 16), :], meta.at[side], meta_sem.at[side])
        for side, tiles_of in enumerate((row_tiles, col_tiles))
    ]
    for load in loads:
        load.start()
    for load in loads:
        load.wait()
    for side in range(2):
        codes[pl.ds(side * tiles, tiles), :] = meta[side].astype(jnp.float32)[:, 0, :].astype(jnp.int32)
    to_index = pltpu.make_async_copy(codes, index, index_sem)
    to_index.start()
    out[...] = jnp.zeros(out.shape, out.dtype)
    kept = [kept_rows[o] * 16 + kept_cols[o] for o in range(KEPT)]
    to_index.wait()

    def fetch(number):
        entry = found[number]
        a, b = entry // 4096, (entry // 8) % 512
        slot = number % DEPTH
        return (
            pltpu.make_async_copy(row_tiles.at[a // 4, pl.ds((a % 4) * BLOCK, BLOCK)], left.at[slot], sems.at[0, slot]),
            pltpu.make_async_copy(col_tiles.at[b // 4, pl.ds((b % 4) * BLOCK, BLOCK)], right.at[slot], sems.at[1, slot]),
        )

    def start(number):
        for copy in fetch(number):
            copy.start()

    def search(inner, count):
        lefts = [index[inner, s] for s in range(SLOTS)]
        rights = [index[inner + tiles, s] for s in range(SLOTS)]
        hits = [
            [flag((lefts[a] != NONE) & ((lefts[a] & 15) == (rights[b] >> 4))) for b in range(SLOTS)] for a in range(SLOTS)
        ]

        def collect(count):
            for a in range(SLOTS):
                for b in range(SLOTS):
                    wanted = (lefts[a] & 240) | (rights[b] & 15)

                    def record(count, a=a, b=b, wanted=wanted):
                        for o in range(KEPT):
                            is_kept = kept[o] == wanted

                            @pl.when(is_kept)
                            def _(count=count, o=o):
                                found[count] = (inner * 4 + a) * 4096 + (inner * 4 + b) * 8 + o

                                @pl.when(count < DEPTH)
                                def _():
                                    start(count)

                            count = count + flag(is_kept)
                        return count

                    count = lax.cond(hits[a][b] == 1, record, lambda count: count, count)
            return count

        any_hit = sum(hits[a][b] for a in range(SLOTS) for b in range(SLOTS))
        return lax.cond(any_hit > 0, collect, lambda count: count, count)

    total = lax.fori_loop(0, tiles, search, 0)

    def work(number, carry):
        slot = number % DEPTH
        for copy in fetch(number):
            copy.wait()
        o = found[number] % 8
        out[o] += jnp.dot(left[slot], right[slot], preferred_element_type=jnp.float32)

        @pl.when(number + DEPTH < total)
        def _():
            start(number + DEPTH)

        return carry

    lax.fori_loop(0, total, work, 0)


def body(p_blocks, p_rows, p_cols, p_count, kept_rows, kept_cols):
    tiles = 32
    anywhere = pl.BlockSpec(memory_space=pl.ANY)
    scalars = pl.BlockSpec(memory_space=pltpu.SMEM)
    tile_list = jax.ShapeDtypeStruct((tiles, TILE, BLOCK), jnp.bfloat16)
    row_tiles, col_tiles = pl.pallas_call(
        gather_kernel,
        out_shape=(tile_list, tile_list),
        in_specs=[scalars, scalars, scalars, anywhere],
        out_specs=(anywhere, anywhere),
        scratch_shapes=[
            pltpu.VMEM((16, BLOCK), jnp.bfloat16),
            pltpu.SemaphoreType.DMA((tiles,)),
            pltpu.SemaphoreType.DMA((tiles, 2)),
            pltpu.SemaphoreType.DMA,
            pltpu.SemaphoreType.DMA((4,)),
            pltpu.SemaphoreType.DMA((6,)),
            pltpu.SemaphoreType.DMA((tiles,)),
            pltpu.SemaphoreType.DMA((tiles,)),
            pltpu.SemaphoreType.DMA((2, 30)),
            pltpu.SemaphoreType.REGULAR,
            pltpu.SemaphoreType.REGULAR,
            pltpu.SemaphoreType.REGULAR,
        ],
        compiler_params=pltpu.CompilerParams(collective_id=0, has_side_effects=True),
        name="gather_tiles",
    )(p_rows.reshape(SLOTS), p_cols.reshape(SLOTS), p_count.reshape(1), p_blocks.reshape(META, BLOCK))
    result = pl.pallas_call(
        multiply_kernel,
        out_shape=jax.ShapeDtypeStruct((KEPT, BLOCK, BLOCK), jnp.float32),
        in_specs=[scalars, scalars, anywhere, anywhere],
        out_specs=pl.BlockSpec(memory_space=pltpu.VMEM),
        scratch_shapes=[
            pltpu.VMEM((2, tiles, 16, BLOCK), jnp.bfloat16),
            pltpu.VMEM((2 * tiles, BLOCK), jnp.int32),
            pltpu.SMEM((2 * tiles, BLOCK), jnp.int32),
            pltpu.SMEM((tiles * SLOTS * KEPT,), jnp.int32),
            pltpu.VMEM((DEPTH, BLOCK, BLOCK), jnp.bfloat16),
            pltpu.VMEM((DEPTH, BLOCK, BLOCK), jnp.bfloat16),
            pltpu.SemaphoreType.DMA((2,)),
            pltpu.SemaphoreType.DMA,
            pltpu.SemaphoreType.DMA((2, DEPTH)),
        ],
        compiler_params=pltpu.CompilerParams(vmem_limit_bytes=16 * 2**20),
        name="multiply_pairs",
    )(kept_rows.reshape(KEPT), kept_cols.reshape(KEPT), row_tiles, col_tiles)
    return result[None, None]


def solution(mesh):
    placed = (
        P("row", "col", None, None, None),
        P("row", "col", None),
        P("row", "col", None),
        P("row", "col"),
        P("row", "col", None),
        P("row", "col", None),
    )
    return jax.shard_map(
        body,
        mesh=mesh,
        in_specs=placed,
        out_specs=P("row", "col", None, None, None),
        check_vma=False,
    )
```

```python
import functools

import jax
import jax.numpy as jnp
from jax import lax
from jax.experimental import pallas as pl
from jax.experimental.pallas import tpu as pltpu
from jax.sharding import PartitionSpec as P

MESH = pl.DeviceIdType.MESH
BLOCK = 128
SLOTS = 3
KEPT = 6
META = SLOTS * BLOCK
TILE = META + 16
HALF = 208
HALVES = ((0, HALF), (HALF, TILE - HALF))
PIECES = ((0, 128), (128, 128), (256, TILE - 256))
RUN = 16
NO_ROW, NO_COL = 20, 30


def device(z_hi, x, y, k, core):
    return (z_hi * 16 + x * 4 + y, k * 2 + core)


def turn(value, by):
    return lax.rem(value + by, 4)


def flag(condition):
    return jnp.where(condition, 1, 0)


def square_kernel(
    p_rows, p_cols, p_count, kept_rows, kept_cols, blocks, out,
    row_tiles, col_tiles, chosen, meta, row_recv, col_recv, anti_recv, own_sem, send_own, send_row, send_pair, send_xy,
    ready_pair, ready_anti,
):
    row, col = lax.axis_index("row"), lax.axis_index("col")
    z_hi, x, y = row // 16, (row // 4) % 4, row % 4
    k, core = col // 2, col % 2
    here = functools.partial(device, z_hi, x, y)
    in_plane = lambda nx, ny: device(z_hi, nx, ny, k, core)
    pair = here(k, 1 - core)
    antipode = device(1 - z_hi, x, y, k, core)

    def signal(semaphore, target):
        pl.semaphore_signal(semaphore, inc=1, device_id=target, device_id_type=MESH)

    first_plane = (z_hi == 0) & (k == 0)
    is_late = first_plane & (x == 0) & (y == 0) & (core == 0)
    late_pair = first_plane & (x == 0) & (y == 0) & (core == 1)
    late_plane = first_plane & (core == 0) & ((x == 0) != (y == 0))

    copies = []

    def local(src, dst, number):
        copy = pltpu.make_async_copy(src, dst, own_sem.at[number])
        copy.start()
        copies.append(copy)

    mine_row, mine_col = row_tiles.at[col], col_tiles.at[row]
    local(blocks, mine_row.at[pl.ds(0, META)], 0)
    local(blocks, mine_col.at[pl.ds(0, META)], 1)

    barrier = pltpu.get_barrier_semaphore()

    @pl.when((core == 0) & (k > 0))
    def _():
        for other in range(2):
            signal(barrier, here(k - 1, other))

    @pl.when((core == 1) & (k < RUN - 1))
    def _():
        for other in range(2):
            signal(barrier, here(k + 1, other))

    @pl.when(jnp.logical_not(is_late))
    def _():
        signal(barrier, pair)
        for d in range(1, 4):
            signal(barrier, in_plane(turn(x, d), y))
            signal(barrier, in_plane(x, turn(y, d)))

    @pl.when(z_hi == 0)
    def _():
        signal(barrier, antipode)

    @pl.when((z_hi == 0) & (core == 1) & (k == 3))
    def _():
        for source in range(8, 16):
            for other in range(2):
                signal(barrier, here(source, other))

    line = lax.broadcasted_iota(jnp.int32, (16, BLOCK), 0)
    codes = jnp.zeros((16, BLOCK), jnp.int32)
    for slot in range(SLOTS):
        used = slot < p_count[0]
        codes = jnp.where(line == slot, jnp.where(used, p_rows[slot], NO_ROW), codes)
        codes = jnp.where(line == SLOTS + slot, jnp.where(used, p_cols[slot], NO_COL), codes)
    meta[...] = codes.astype(jnp.float32).astype(jnp.bfloat16)
    local(meta, mine_row.at[pl.ds(META, 16)], 2)
    local(meta, mine_col.at[pl.ds(META, 16)], 3)

    expected = (
        flag(k < RUN - 1) + flag(k > 0) + 1 - flag(late_pair) + 6 - flag(late_plane) + flag((z_hi == 0) & (k >= 8)) + z_hi
    )
    pl.semaphore_wait(barrier, expected)

    @pl.when(z_hi == 1)
    def _():
        signal(ready_anti, antipode)

    @pl.when(is_late)
    def _():
        signal(ready_pair, pair)
        for d in range(1, 4):
            signal(ready_pair, in_plane(turn(x, d), y))
            signal(ready_pair, in_plane(x, turn(y, d)))

    for copy in copies:
        copy.wait()

    def send(src, dst, send_sem, recv_sem, target):
        return pltpu.make_async_remote_copy(
            src_ref=src, dst_ref=dst, send_sem=send_sem, recv_sem=recv_sem, device_id=target, device_id_type=MESH
        )

    def pair_send(tile):
        return send(row_tiles.at[tile], row_tiles.at[tile], send_pair.at[tile], row_recv.at[tile, 0], pair)

    def piece_sends(tile, send_sem, target):
        parts = [row_tiles.at[tile, pl.ds(low, size)] for low, size in PIECES]
        return [send(part, part, send_sem.at[n], row_recv.at[tile, n], target) for n, part in enumerate(parts)]

    anti_send = send(mine_col, mine_col, own_sem.at[4], anti_recv, antipode)
    own_sends = (
        (k > 0, piece_sends(col, send_own.at[0], here(k - 1, 1))),
        (k < RUN - 1, piece_sends(col, send_own.at[1], here(k + 1, 0))),
        ((z_hi == 0) & (k >= 8), piece_sends(col, send_own.at[2], here(3, 1))),
    )

    @pl.when(z_hi == 1)
    def _():
        anti_send.start()

    for wanted, sends in own_sends:

        @pl.when(wanted)
        def _(sends=sends):
            for copy in sends:
                copy.start()

    def half_send(side, tile, half, number, target):
        low, size = HALVES[half]
        part = col_tiles.at[tile, pl.ds(low, size)]
        return send(part, part, send_xy.at[side, number], col_recv.at[tile, half], target)

    def plane_tile(side, nx, ny):
        z = z_hi if side == 0 else 1 - z_hi
        return z * 16 + nx * 4 + ny

    def plane_own(side):
        mine = plane_tile(side, x, y)
        return [
            half_send(side, mine, half, number * 6 + (d - 1) * 2 + half, in_plane(turn(x, d), y) if along_x else in_plane(x, turn(y, d)))
            for number in range(2)
            for d in (2, 1, 3)
            for half in range(2)
            for along_x in ((half == 0) == (number == 0),)
        ]

    def plane_forward(side, d):
        from_x = plane_tile(side, turn(x, 4 - d), y)
        from_y = plane_tile(side, x, turn(y, 4 - d))
        first = [half_send(side, from_x, 0, 12 + (d - 1) * 6 + e - 1, in_plane(x, turn(y, e))) for e in (2, 1, 3)]
        second = [half_send(side, from_y, 1, 15 + (d - 1) * 6 + e - 1, in_plane(turn(x, e), y)) for e in (2, 1, 3)]
        return first, second

    def arrived(side, tile, half):
        half_send(side, tile, half, 0, pair).wait_recv()

    def plane_first(side):
        for copy in plane_own(side):
            copy.start()

    def plane_second(side):
        for d in (1, 3, 2):
            first, second = plane_forward(side, d)
            arrived(side, plane_tile(side, turn(x, 4 - d), y), 0)
            for copy in first:
                copy.start()
            arrived(side, plane_tile(side, x, turn(y, 4 - d)), 1)
            for copy in second:
                copy.start()

    def plane_sent(side):
        for copy in plane_own(side):
            copy.wait_send()
        for d in range(1, 4):
            for copies_of in plane_forward(side, d):
                for copy in copies_of:
                    copy.wait_send()

    @pl.when(late_plane)
    def _():
        pl.semaphore_wait(ready_pair, 1)

    plane_first(0)

    @pl.when(late_pair)
    def _():
        pl.semaphore_wait(ready_pair, 1)

    pair_send(col).start()
    plane_second(0)

    step = 2 * core - 1
    onward = here(jnp.clip(k - step, 0, RUN - 1), core)

    def is_valid(source):
        return (source >= 0) & (source < RUN)

    def goes_on(source):
        left = (k > 0) & jnp.logical_not((z_hi == 0) & (k == 4) & (source >= 8))
        return jnp.where(core == 0, flag(k < RUN - 1), flag(left)) == 1

    anti_at, anti_next = 7, 9

    def anti_first():
        @pl.when(z_hi == 0)
        def _():
            pl.semaphore_wait(ready_anti, 1)
            anti_send.start()

        anti_send.wait_recv()
        plane_first(1)

    def stream(t, carry):
        source = k + step * t

        @pl.when(is_valid(source))
        def _():
            goes = goes_on(source)
            for other in range(2):
                tile = source * 2 + other
                for copy in piece_sends(tile, send_row.at[tile], onward):
                    copy.wait_recv()
                    pl.when(goes)(copy.start)
                pair_send(tile).start()

        @pl.when(t == anti_at)
        def _():
            anti_first()

        @pl.when(t == anti_next)
        def _():
            plane_second(1)

        return carry

    lax.fori_loop(1, RUN, stream, 0)

    out[...] = jnp.zeros(out.shape, out.dtype)

    def spread(tiles, tile, number):
        line_of = tiles[tile, pl.ds(META, 16), :].astype(jnp.float32)[number : number + 1, :]
        return jnp.broadcast_to(line_of, (16, BLOCK))

    def weight(condition):
        return jnp.where(condition, 1.0, 0.0).astype(jnp.float32)

    def multiply(n, carry):
        tile = jnp.where(n < 16, z_hi * 16 + n, (1 - z_hi) * 16 + n - 16)
        source, other = tile // 2, tile % 2
        side = flag(n >= 16)
        nx, ny = (tile // 4) % 4, tile % 4
        own_x, own_y = nx == x, ny == y

        @pl.when(((source - k) * step < 0) | ((source == k) & (other != core)))
        def _():
            pair_send(tile).wait_recv()

        @pl.when(jnp.logical_not(own_y))
        def _():
            arrived(side, tile, 0)

        @pl.when(jnp.logical_not(own_x))
        def _():
            arrived(side, tile, 1)

        left_rows = [spread(row_tiles, tile, s) for s in range(SLOTS)]
        left_cols = [spread(row_tiles, tile, SLOTS + s) for s in range(SLOTS)]
        right_rows = [spread(col_tiles, tile, s) for s in range(SLOTS)]
        right_cols = [spread(col_tiles, tile, SLOTS + s) for s in range(SLOTS)]
        inner = [[weight(left_cols[a] == right_rows[b]) for b in range(SLOTS)] for a in range(SLOTS)]
        for o in range(KEPT):
            in_row = [weight(left_rows[a] == kept_rows[o].astype(jnp.float32)) for a in range(SLOTS)]
            in_col = [weight(right_cols[b] == kept_cols[o].astype(jnp.float32)) for b in range(SLOTS)]
            for b in range(SLOTS):
                factors = [(in_row[a] * in_col[b] * inner[a][b]).astype(jnp.bfloat16) for a in range(SLOTS)]
                for low in range(0, BLOCK, 16):
                    terms = [factors[a] * row_tiles[tile, pl.ds(a * BLOCK + low, 16), :] for a in range(SLOTS)]
                    chosen[pl.ds(o * BLOCK + low, 16), pl.ds(b * BLOCK, BLOCK)] = terms[0] + terms[1] + terms[2]
        out[...] += jnp.dot(chosen[...], col_tiles[tile, pl.ds(0, META), :], preferred_element_type=jnp.float32)
        return carry

    lax.fori_loop(0, 32, multiply, 0)

    def settle(t, carry):
        source = k + step * t

        @pl.when(is_valid(source))
        def _():
            goes = goes_on(source)
            for other in range(2):
                tile = source * 2 + other
                for copy in piece_sends(tile, send_row.at[tile], onward):
                    pl.when(goes)(copy.wait_send)
                pair_send(tile).wait_send()

        return carry

    lax.fori_loop(1, RUN, settle, 0)
    plane_sent(0)
    plane_sent(1)
    anti_send.wait_send()
    pair_send(col).wait_send()
    for wanted, sends in own_sends:

        @pl.when(wanted)
        def _(sends=sends):
            for copy in sends:
                copy.wait_send()


def body(p_blocks, p_rows, p_cols, p_count, kept_rows, kept_cols):
    tiles = 32
    scalars = pl.BlockSpec(memory_space=pltpu.SMEM)
    result = pl.pallas_call(
        square_kernel,
        out_shape=jax.ShapeDtypeStruct((KEPT * BLOCK, BLOCK), jnp.float32),
        in_specs=[scalars] * 5 + [pl.BlockSpec(memory_space=pl.ANY)],
        out_specs=pl.BlockSpec(memory_space=pltpu.VMEM),
        scratch_shapes=[
            pltpu.VMEM((tiles, TILE, BLOCK), jnp.bfloat16),
            pltpu.VMEM((tiles, TILE, BLOCK), jnp.bfloat16),
            pltpu.VMEM((KEPT * BLOCK, META), jnp.bfloat16),
            pltpu.VMEM((16, BLOCK), jnp.bfloat16),
            pltpu.SemaphoreType.DMA((tiles, 3)),
            pltpu.SemaphoreType.DMA((tiles, 2)),
            pltpu.SemaphoreType.DMA,
            pltpu.SemaphoreType.DMA((5,)),
            pltpu.SemaphoreType.DMA((3, 3)),
            pltpu.SemaphoreType.DMA((tiles, 3)),
            pltpu.SemaphoreType.DMA((tiles,)),
            pltpu.SemaphoreType.DMA((2, 30)),
            pltpu.SemaphoreType.REGULAR,
            pltpu.SemaphoreType.REGULAR,
        ],
        compiler_params=pltpu.CompilerParams(collective_id=0, has_side_effects=True, vmem_limit_bytes=24 * 2**20),
        name="square_blocks",
    )(
        p_rows.reshape(SLOTS), p_cols.reshape(SLOTS), p_count.reshape(1), kept_rows.reshape(KEPT), kept_cols.reshape(KEPT),
        p_blocks.reshape(META, BLOCK),
    )
    return result.reshape(1, 1, KEPT, BLOCK, BLOCK)


def solution(mesh):
    placed = (
        P("row", "col", None, None, None),
        P("row", "col", None),
        P("row", "col", None),
        P("row", "col"),
        P("row", "col", None),
        P("row", "col", None),
    )
    return jax.shard_map(
        body,
        mesh=mesh,
        in_specs=placed,
        out_specs=P("row", "col", None, None, None),
        check_vma=False,
    )
```

```python
import functools

import jax
import jax.numpy as jnp
from jax import lax
from jax.experimental import pallas as pl
from jax.experimental.pallas import tpu as pltpu
from jax.sharding import PartitionSpec as P

MESH = pl.DeviceIdType.MESH
BLOCK = 128
SLOTS = 3
KEPT = 6
META = SLOTS * BLOCK
TILE = META + 16
HALF = 208
HALVES = ((0, HALF), (HALF, TILE - HALF))
PIECES = ((0, 128), (128, 128), (256, TILE - 256))
RUN = 16
NO_ROW, NO_COL = 20, 30
ANTI_T, ANTI_D, READY_T, MULTIPLY_T = 7, 2, 5, 6


def device(z_hi, x, y, k, core):
    return (z_hi * 16 + x * 4 + y, k * 2 + core)


def turn(value, by):
    return lax.rem(value + by, 4)


def flag(condition):
    return jnp.where(condition, 1, 0)


def square_kernel(
    p_rows, p_cols, p_count, kept_rows, kept_cols, blocks, out,
    row_tiles, col_tiles, chosen, meta, row_recv, col_recv, anti_recv, own_sem, send_own, send_anti, send_row, send_pair, send_xy,
    ready_pair, ready_anti,
):
    row, col = lax.axis_index("row"), lax.axis_index("col")
    z_hi, x, y = row // 16, (row // 4) % 4, row % 4
    k, core = col // 2, col % 2
    here = functools.partial(device, z_hi, x, y)
    in_plane = lambda nx, ny: device(z_hi, nx, ny, k, core)
    pair = here(k, 1 - core)
    antipode = device(1 - z_hi, x, y, k, core)

    def signal(semaphore, target):
        pl.semaphore_signal(semaphore, inc=1, device_id=target, device_id_type=MESH)

    first_plane = (z_hi == 0) & (k == 0)
    is_late = first_plane & (x == 0) & (y == 0) & (core == 0)
    late_pair = first_plane & (x == 0) & (y == 0) & (core == 1)
    late_plane = first_plane & (core == 0) & ((x == 0) != (y == 0))

    copies = []

    def local(src, dst, number):
        copy = pltpu.make_async_copy(src, dst, own_sem.at[number])
        copy.start()
        copies.append(copy)

    mine_row, mine_col = row_tiles.at[col], col_tiles.at[row]
    local(blocks, mine_row.at[pl.ds(0, META)], 0)
    local(blocks, mine_col.at[pl.ds(0, META)], 1)

    barrier = pltpu.get_barrier_semaphore()

    @pl.when((core == 0) & (k > 0))
    def _():
        for other in range(2):
            signal(barrier, here(k - 1, other))

    @pl.when((core == 1) & (k < RUN - 1))
    def _():
        for other in range(2):
            signal(barrier, here(k + 1, other))

    @pl.when(jnp.logical_not(is_late))
    def _():
        signal(barrier, pair)
        for d in range(1, 4):
            signal(barrier, in_plane(turn(x, d), y))
            signal(barrier, in_plane(x, turn(y, d)))

    at_end = (k == 0) | (k == RUN - 1)
    agent = ((k == 0) & (core == 1)) | ((k == RUN - 1) & (core == 0))
    anti_count = flag(at_end) + 14 * flag(agent)
    near_end = jnp.where(k < 8, 0, RUN - 1)
    anti_source = device(1 - z_hi, x, y, near_end, jnp.where(at_end, core, jnp.where(k < 8, 1, 0)))
    across = functools.partial(device, 1 - z_hi, x, y)

    @pl.when(z_hi == 0)
    def _():
        signal(barrier, anti_source)

        @pl.when(at_end)
        def _():
            signal(barrier, antipode)

        @pl.when(agent)
        def _():
            for distance in range(1, 8):
                for other in range(2):
                    signal(barrier, across(jnp.where(core == 1, distance, RUN - 1 - distance), other))

    line = lax.broadcasted_iota(jnp.int32, (16, BLOCK), 0)
    codes = jnp.zeros((16, BLOCK), jnp.int32)
    for slot in range(SLOTS):
        used = slot < p_count[0]
        codes = jnp.where(line == slot, jnp.where(used, p_rows[slot], NO_ROW), codes)
        codes = jnp.where(line == SLOTS + slot, jnp.where(used, p_cols[slot], NO_COL), codes)
    meta[...] = codes.astype(jnp.float32).astype(jnp.bfloat16)
    local(meta, mine_row.at[pl.ds(META, 16)], 2)
    local(meta, mine_col.at[pl.ds(META, 16)], 3)

    expected = (
        flag(k < RUN - 1) + flag(k > 0) + 1 - flag(late_pair) + 6 - flag(late_plane) + z_hi * (1 + anti_count)
    )
    pl.semaphore_wait(barrier, expected)

    @pl.when(z_hi == 1)
    def _():
        signal(ready_anti, anti_source)

    @pl.when(is_late)
    def _():
        signal(ready_pair, pair)
        for d in range(1, 4):
            signal(ready_pair, in_plane(turn(x, d), y))
            signal(ready_pair, in_plane(x, turn(y, d)))

    for copy in copies:
        copy.wait()

    def send(src, dst, send_sem, recv_sem, target):
        return pltpu.make_async_remote_copy(
            src_ref=src, dst_ref=dst, send_sem=send_sem, recv_sem=recv_sem, device_id=target, device_id_type=MESH
        )

    def pair_send(tile):
        return send(row_tiles.at[tile], row_tiles.at[tile], send_pair.at[tile], row_recv.at[tile, 0], pair)

    def piece_sends(tile, send_sem, target):
        parts = [row_tiles.at[tile, pl.ds(low, size)] for low, size in PIECES]
        return [send(part, part, send_sem.at[n], row_recv.at[tile, n], target) for n, part in enumerate(parts)]

    anti_send = send(mine_col, mine_col, own_sem.at[4], anti_recv, antipode)
    own_sends = (
        (k > 0, piece_sends(col, send_own.at[0], here(k - 1, 1))),
        (k < RUN - 1, piece_sends(col, send_own.at[1], here(k + 1, 0))),
    )

    @pl.when((z_hi == 1) & at_end)
    def _():
        anti_send.start()

    for wanted, sends in own_sends:

        @pl.when(wanted)
        def _(sends=sends):
            for copy in sends:
                copy.start()

    def half_send(side, tile, half, number, target):
        low, size = HALVES[half]
        part = col_tiles.at[tile, pl.ds(low, size)]
        return send(part, part, send_xy.at[side, number], col_recv.at[tile, half], target)

    def plane_tile(side, nx, ny):
        z = z_hi if side == 0 else 1 - z_hi
        return z * 16 + nx * 4 + ny

    def plane_own(side):
        mine = plane_tile(side, x, y)
        return [
            half_send(side, mine, half, number * 6 + (d - 1) * 2 + half, in_plane(turn(x, d), y) if along_x else in_plane(x, turn(y, d)))
            for number in range(2)
            for d in (2, 1, 3)
            for half in range(2)
            for along_x in ((half == 0) == (number == 0),)
        ]

    def plane_forward(side, d):
        from_x = plane_tile(side, turn(x, 4 - d), y)
        from_y = plane_tile(side, x, turn(y, 4 - d))
        first = [half_send(side, from_x, 0, 12 + (d - 1) * 6 + e - 1, in_plane(x, turn(y, e))) for e in (2, 1, 3)]
        second = [half_send(side, from_y, 1, 15 + (d - 1) * 6 + e - 1, in_plane(turn(x, e), y)) for e in (2, 1, 3)]
        return first, second

    def arrived(side, tile, half):
        half_send(side, tile, half, 0, pair).wait_recv()

    def plane_first(side):
        for copy in plane_own(side):
            copy.start()

    def plane_second(side):
        for d in (1, 3, 2):
            first, second = plane_forward(side, d)
            arrived(side, plane_tile(side, turn(x, 4 - d), y), 0)
            for copy in first:
                copy.start()
            arrived(side, plane_tile(side, x, turn(y, 4 - d)), 1)
            for copy in second:
                copy.start()

    def plane_sent(side):
        for copy in plane_own(side):
            copy.wait_send()
        for d in range(1, 4):
            for copies_of in plane_forward(side, d):
                for copy in copies_of:
                    copy.wait_send()

    @pl.when(late_plane)
    def _():
        pl.semaphore_wait(ready_pair, 1)

    plane_first(0)

    @pl.when(late_pair)
    def _():
        pl.semaphore_wait(ready_pair, 1)

    pair_send(col).start()
    plane_second(0)

    step = 2 * core - 1
    onward = here(jnp.clip(k - step, 0, RUN - 1), core)

    def is_valid(source):
        return (source >= 0) & (source < RUN)

    def goes_on(source):
        return jnp.where(core == 0, k, RUN - 1 - k) < RUN - 1

    to_end = jnp.where(core == 0, RUN - 1 - k, k)
    anti_at = jnp.minimum(ANTI_T + to_end // 2, RUN - 2)
    anti_next = jnp.minimum(anti_at + ANTI_D, RUN - 1)

    def across_send(distance, other):
        source = k + step * distance
        tile = source * 2 + other
        target = across(source, other)
        return send(row_tiles.at[tile], col_tiles.at[row], send_anti.at[distance * 2 + other], anti_recv, target)

    def across_start(distance):
        for other in range(2):
            across_send(distance, other).start()

    def anti_first():
        anti_send.wait_recv()
        plane_first(1)

    out[...] = jnp.zeros(out.shape, out.dtype)

    def spread(tiles, tile, number):
        line_of = tiles[tile, pl.ds(META, 16), :].astype(jnp.float32)[number : number + 1, :]
        return jnp.broadcast_to(line_of, (16, BLOCK))

    def weight(condition):
        return jnp.where(condition, 1.0, 0.0).astype(jnp.float32)

    def multiply(tile):
        side = flag(tile // 16 != z_hi)
        own_x, own_y = (tile // 4) % 4 == x, tile % 4 == y

        @pl.when(jnp.logical_not(own_y))
        def _():
            arrived(side, tile, 0)

        @pl.when(jnp.logical_not(own_x))
        def _():
            arrived(side, tile, 1)

        left_rows = [spread(row_tiles, tile, s) for s in range(SLOTS)]
        left_cols = [spread(row_tiles, tile, SLOTS + s) for s in range(SLOTS)]
        right_rows = [spread(col_tiles, tile, s) for s in range(SLOTS)]
        right_cols = [spread(col_tiles, tile, SLOTS + s) for s in range(SLOTS)]
        inner = [[weight(left_cols[a] == right_rows[b]) for b in range(SLOTS)] for a in range(SLOTS)]
        for o in range(KEPT):
            in_row = [weight(left_rows[a] == kept_rows[o].astype(jnp.float32)) for a in range(SLOTS)]
            in_col = [weight(right_cols[b] == kept_cols[o].astype(jnp.float32)) for b in range(SLOTS)]
            for b in range(SLOTS):
                factors = [(in_row[a] * in_col[b] * inner[a][b]).astype(jnp.bfloat16) for a in range(SLOTS)]
                for low in range(0, BLOCK, 16):
                    terms = [factors[a] * row_tiles[tile, pl.ds(a * BLOCK + low, 16), :] for a in range(SLOTS)]
                    chosen[pl.ds(o * BLOCK + low, 16), pl.ds(b * BLOCK, BLOCK)] = terms[0] + terms[1] + terms[2]
        out[...] += jnp.dot(chosen[...], col_tiles[tile, pl.ds(0, META), :], preferred_element_type=jnp.float32)

    def is_early(source, t):
        return (source // 8 == z_hi) | (t > anti_next + 1)

    def multiply_early(t, number):
        place = jnp.maximum((t - MULTIPLY_T) * 3 + number, 0)
        source = k + step * (place // 2 + 1)

        @pl.when((t >= MULTIPLY_T) & is_valid(source) & is_early(source, t))
        def _():
            multiply(source * 2 + place % 2)

    def stream(t, carry):
        source = k + step * t

        def part(other, carry):
            @pl.when(is_valid(source))
            def _():
                goes = goes_on(source)
                tile = source * 2 + other
                for copy in piece_sends(tile, send_row.at[tile], onward):
                    copy.wait_recv()
                    pl.when(goes)(copy.start)
                pair_send(tile).start()

            def between(n, carry):
                multiply_early(t, other + n)
                return carry

            return lax.fori_loop(0, 1 + other, between, carry)

        lax.fori_loop(0, 2, part, 0)

        @pl.when(agent & (t < 8) & ((z_hi == 1) | (t > READY_T)))
        def _():
            across_start(t)

        @pl.when(at_end & (z_hi == 0) & (t == READY_T))
        def _():
            pl.semaphore_wait(ready_anti, anti_count)
            anti_send.start()

            @pl.when(agent)
            def _():
                for distance in range(1, READY_T + 1):
                    across_start(distance)

        @pl.when(t == anti_at)
        def _():
            anti_first()

        @pl.when(t == anti_next)
        def _():
            plane_second(1)

        return carry

    lax.fori_loop(1, RUN, stream, 0)

    def rest(n, carry):
        tile = jnp.where(n < 16, z_hi * 16 + n, (1 - z_hi) * 16 + n - 16)
        source, other = tile // 2, tile % 2
        distance = (source - k) * step
        by_pair = (distance < 0) | ((distance == 0) & (other != core))
        done = (distance > 0) & is_early(source, MULTIPLY_T + ((distance - 1) * 2 + other) // 3)

        @pl.when(by_pair)
        def _():
            pair_send(tile).wait_recv()

        @pl.when(jnp.logical_not(done))
        def _():
            multiply(tile)

        return carry

    lax.fori_loop(0, 32, rest, 0)

    def settle(t, carry):
        source = k + step * t

        @pl.when(is_valid(source))
        def _():
            goes = goes_on(source)
            for other in range(2):
                tile = source * 2 + other
                for copy in piece_sends(tile, send_row.at[tile], onward):
                    pl.when(goes)(copy.wait_send)
                pair_send(tile).wait_send()

        return carry

    lax.fori_loop(1, RUN, settle, 0)
    plane_sent(0)
    plane_sent(1)
    pl.when(at_end)(anti_send.wait_send)

    @pl.when(agent)
    def _():
        for distance in range(1, 8):
            for other in range(2):
                across_send(distance, other).wait_send()

    pair_send(col).wait_send()
    for wanted, sends in own_sends:

        @pl.when(wanted)
        def _(sends=sends):
            for copy in sends:
                copy.wait_send()


def body(p_blocks, p_rows, p_cols, p_count, kept_rows, kept_cols):
    tiles = 32
    scalars = pl.BlockSpec(memory_space=pltpu.SMEM)
    result = pl.pallas_call(
        square_kernel,
        out_shape=jax.ShapeDtypeStruct((KEPT * BLOCK, BLOCK), jnp.float32),
        in_specs=[scalars] * 5 + [pl.BlockSpec(memory_space=pl.ANY)],
        out_specs=pl.BlockSpec(memory_space=pltpu.VMEM),
        scratch_shapes=[
            pltpu.VMEM((tiles, TILE, BLOCK), jnp.bfloat16),
            pltpu.VMEM((tiles, TILE, BLOCK), jnp.bfloat16),
            pltpu.VMEM((KEPT * BLOCK, META), jnp.bfloat16),
            pltpu.VMEM((16, BLOCK), jnp.bfloat16),
            pltpu.SemaphoreType.DMA((tiles, 3)),
            pltpu.SemaphoreType.DMA((tiles, 2)),
            pltpu.SemaphoreType.DMA,
            pltpu.SemaphoreType.DMA((5,)),
            pltpu.SemaphoreType.DMA((2, 3)),
            pltpu.SemaphoreType.DMA((16,)),
            pltpu.SemaphoreType.DMA((tiles, 3)),
            pltpu.SemaphoreType.DMA((tiles,)),
            pltpu.SemaphoreType.DMA((2, 30)),
            pltpu.SemaphoreType.REGULAR,
            pltpu.SemaphoreType.REGULAR,
        ],
        compiler_params=pltpu.CompilerParams(collective_id=0, has_side_effects=True, vmem_limit_bytes=24 * 2**20),
        name="square_blocks",
    )(
        p_rows.reshape(SLOTS), p_cols.reshape(SLOTS), p_count.reshape(1), kept_rows.reshape(KEPT), kept_cols.reshape(KEPT),
        p_blocks.reshape(META, BLOCK),
    )
    return result.reshape(1, 1, KEPT, BLOCK, BLOCK)


def solution(mesh):
    placed = (
        P("row", "col", None, None, None),
        P("row", "col", None),
        P("row", "col", None),
        P("row", "col"),
        P("row", "col", None),
        P("row", "col", None),
    )
    return jax.shard_map(
        body,
        mesh=mesh,
        in_specs=placed,
        out_specs=P("row", "col", None, None, None),
        check_vma=False,
    )
```

```python
import functools

import jax
import jax.numpy as jnp
from jax import lax
from jax.experimental import pallas as pl
from jax.experimental.pallas import tpu as pltpu
from jax.sharding import PartitionSpec as P

MESH = pl.DeviceIdType.MESH
BLOCK = 128
SLOTS = 3
KEPT = 6
META = SLOTS * BLOCK
TILE = META + 16
HALF = 208
HALVES = ((0, HALF), (HALF, TILE - HALF))
NEAR = 3
RIGHT_FROM = 7
PIECES = ((0, 128), (128, 128), (256, TILE - 256))
RUN = 16
NO_ROW, NO_COL = 20, 30
ANTI_D, READY_T, MULTIPLY_T = 2, 6, 6


def device(z_hi, x, y, k, core):
    return (z_hi * 16 + x * 4 + y, k * 2 + core)


def turn(value, by):
    return lax.rem(value + by, 4)


def flag(condition):
    return jnp.where(condition, 1, 0)


def square_kernel(
    p_rows, p_cols, p_count, kept_rows, kept_cols, blocks, out,
    row_tiles, col_tiles, chosen, meta, row_recv, col_recv, anti_recv, own_sem, send_own, send_anti, send_row, send_pair, send_xy,
    ready_pair, ready_anti,
):
    row, col = lax.axis_index("row"), lax.axis_index("col")
    z_hi, x, y = row // 16, (row // 4) % 4, row % 4
    k, core = col // 2, col % 2
    here = functools.partial(device, z_hi, x, y)
    in_plane = lambda nx, ny: device(z_hi, nx, ny, k, core)
    pair = here(k, 1 - core)
    antipode = device(1 - z_hi, x, y, k, core)

    def signal(semaphore, target):
        pl.semaphore_signal(semaphore, inc=1, device_id=target, device_id_type=MESH)

    first_plane = (z_hi == 0) & (k == 0)
    is_late = first_plane & (x == 0) & (y == 0) & (core == 0)
    late_pair = first_plane & (x == 0) & (y == 0) & (core == 1)
    late_plane = first_plane & (core == 0) & ((x == 0) != (y == 0))

    copies = []

    def local(src, dst, number):
        copy = pltpu.make_async_copy(src, dst, own_sem.at[number])
        copy.start()
        copies.append(copy)

    mine_row, mine_col = row_tiles.at[col], col_tiles.at[row]
    local(blocks, mine_row.at[pl.ds(0, META)], 0)
    local(blocks, mine_col.at[pl.ds(0, META)], 1)

    barrier = pltpu.get_barrier_semaphore()

    @pl.when((core == 0) & (k > 0))
    def _():
        for other in range(2):
            signal(barrier, here(k - 1, other))

    @pl.when((core == 1) & (k < RUN - 1))
    def _():
        for other in range(2):
            signal(barrier, here(k + 1, other))

    @pl.when(jnp.logical_not(is_late))
    def _():
        signal(barrier, pair)
        for d in range(1, 4):
            signal(barrier, in_plane(turn(x, d), y))
            signal(barrier, in_plane(x, turn(y, d)))

    at_end = (k == 0) | (k == RUN - 1)
    agent = ((k == 0) & (core == 1)) | ((k == RUN - 1) & (core == 0))
    across_low = jnp.where(z_hi == 0, 8, 1)
    across_high = jnp.where(z_hi == 0, 14 - NEAR, jnp.where(core == 1, RIGHT_FROM - 1, 15 - RIGHT_FROM))
    anti_count = flag(at_end) + flag(agent) * 2 * (across_high - across_low + 1 + NEAR * (1 - z_hi))
    near_left, near_right = k <= NEAR, k >= RUN - 1 - NEAR
    from_left = jnp.where(z_hi == 0, flag(k < RIGHT_FROM), flag(near_left | ((k >= 8) & jnp.logical_not(near_right)))) == 1
    anti_source = device(
        1 - z_hi, x, y,
        jnp.where(at_end, k, jnp.where(from_left, 0, RUN - 1)), jnp.where(at_end, core, jnp.where(from_left, 1, 0)),
    )
    across = functools.partial(device, 1 - z_hi, x, y)

    @pl.when(z_hi == 0)
    def _():
        signal(barrier, anti_source)

        @pl.when(at_end)
        def _():
            signal(barrier, antipode)

        @pl.when(agent)
        def _():
            for distance in (*range(1, NEAR + 1), *range(8, 15 - NEAR)):
                for other in range(2):
                    signal(barrier, across(jnp.where(core == 1, distance, RUN - 1 - distance), other))

    line = lax.broadcasted_iota(jnp.int32, (16, BLOCK), 0)
    codes = jnp.zeros((16, BLOCK), jnp.int32)
    for slot in range(SLOTS):
        used = slot < p_count[0]
        codes = jnp.where(line == slot, jnp.where(used, p_rows[slot], NO_ROW), codes)
        codes = jnp.where(line == SLOTS + slot, jnp.where(used, p_cols[slot], NO_COL), codes)
    meta[...] = codes.astype(jnp.float32).astype(jnp.bfloat16)
    local(meta, mine_row.at[pl.ds(META, 16)], 2)
    local(meta, mine_col.at[pl.ds(META, 16)], 3)

    expected = (
        flag(k < RUN - 1) + flag(k > 0) + 1 - flag(late_pair) + 6 - flag(late_plane) + z_hi * (1 + anti_count)
    )
    pl.semaphore_wait(barrier, expected)

    @pl.when(z_hi == 1)
    def _():
        signal(ready_anti, anti_source)

    @pl.when(is_late)
    def _():
        signal(ready_pair, pair)
        for d in range(1, 4):
            signal(ready_pair, in_plane(turn(x, d), y))
            signal(ready_pair, in_plane(x, turn(y, d)))

    for copy in copies:
        copy.wait()

    def send(src, dst, send_sem, recv_sem, target):
        return pltpu.make_async_remote_copy(
            src_ref=src, dst_ref=dst, send_sem=send_sem, recv_sem=recv_sem, device_id=target, device_id_type=MESH
        )

    def pair_send(tile):
        return send(row_tiles.at[tile], row_tiles.at[tile], send_pair.at[tile], row_recv.at[tile, 0], pair)

    def piece_sends(tile, send_sem, target):
        parts = [row_tiles.at[tile, pl.ds(low, size)] for low, size in PIECES]
        return [send(part, part, send_sem.at[n], row_recv.at[tile, n], target) for n, part in enumerate(parts)]

    anti_send = send(mine_col, mine_col, own_sem.at[4], anti_recv, antipode)
    own_sends = (
        (k > 0, piece_sends(col, send_own.at[0], here(k - 1, 1))),
        (k < RUN - 1, piece_sends(col, send_own.at[1], here(k + 1, 0))),
    )

    @pl.when((z_hi == 1) & at_end)
    def _():
        anti_send.start()

    for wanted, sends in own_sends:

        @pl.when(wanted)
        def _(sends=sends):
            for copy in sends:
                copy.start()

    def half_send(side, tile, half, number, target):
        low, size = HALVES[half]
        part = col_tiles.at[tile, pl.ds(low, size)]
        return send(part, part, send_xy.at[side, number], col_recv.at[tile, half], target)

    def plane_tile(side, nx, ny):
        z = z_hi if side == 0 else 1 - z_hi
        return z * 16 + nx * 4 + ny

    def plane_own(side):
        mine = plane_tile(side, x, y)
        return [
            half_send(side, mine, half, number * 6 + (d - 1) * 2 + half, in_plane(turn(x, d), y) if along_x else in_plane(x, turn(y, d)))
            for number in range(2)
            for d in (2, 1, 3)
            for half in range(2)
            for along_x in ((half == 0) == (number == 0),)
        ]

    def plane_forward(side, d):
        from_x = plane_tile(side, turn(x, 4 - d), y)
        from_y = plane_tile(side, x, turn(y, 4 - d))
        first = [half_send(side, from_x, 0, 12 + (d - 1) * 6 + e - 1, in_plane(x, turn(y, e))) for e in (2, 1, 3)]
        second = [half_send(side, from_y, 1, 15 + (d - 1) * 6 + e - 1, in_plane(turn(x, e), y)) for e in (2, 1, 3)]
        return first, second

    def arrived(side, tile, half):
        half_send(side, tile, half, 0, pair).wait_recv()

    def plane_first(side):
        for copy in plane_own(side):
            copy.start()

    def plane_second(side):
        for d in (1, 3, 2):
            first, second = plane_forward(side, d)
            arrived(side, plane_tile(side, turn(x, 4 - d), y), 0)
            for copy in first:
                copy.start()
            arrived(side, plane_tile(side, x, turn(y, 4 - d)), 1)
            for copy in second:
                copy.start()

    def plane_sent(side):
        for copy in plane_own(side):
            copy.wait_send()
        for d in range(1, 4):
            for copies_of in plane_forward(side, d):
                for copy in copies_of:
                    copy.wait_send()

    @pl.when(late_plane)
    def _():
        pl.semaphore_wait(ready_pair, 1)

    plane_first(0)

    @pl.when(late_pair)
    def _():
        pl.semaphore_wait(ready_pair, 1)

    pair_send(col).start()
    plane_second(0)

    step = 2 * core - 1
    onward = here(jnp.clip(k - step, 0, RUN - 1), core)

    def is_valid(source):
        return (source >= 0) & (source < RUN)

    def goes_on(source):
        return jnp.where(core == 0, k, RUN - 1 - k) < RUN - 1

    late = RUN - 2
    run0_at = jnp.where(core == 1, jnp.where(k < RIGHT_FROM, 7 + k // 2, late), jnp.minimum(5 + 2 * (RUN - 1 - k), late))
    run1_at = jnp.where(at_end, 8, jnp.where(jnp.where(core == 1, flag(near_left), flag(near_right)) == 1, 10, late))
    anti_at = jnp.where(z_hi == 0, run0_at, run1_at)
    anti_next = jnp.minimum(anti_at + ANTI_D, RUN - 1)

    def across_send(distance, other):
        source = k + step * distance
        tile = source * 2 + other
        target = across(source, other)
        return send(row_tiles.at[tile], col_tiles.at[row], send_anti.at[distance * 2 + other], anti_recv, target)

    def across_start(distance):
        for other in range(2):
            across_send(distance, other).start()

    def anti_first():
        anti_send.wait_recv()
        plane_first(1)

    out[...] = jnp.zeros(out.shape, out.dtype)

    def spread(tiles, tile, number):
        line_of = tiles[tile, pl.ds(META, 16), :].astype(jnp.float32)[number : number + 1, :]
        return jnp.broadcast_to(line_of, (16, BLOCK))

    def weight(condition):
        return jnp.where(condition, 1.0, 0.0).astype(jnp.float32)

    def multiply(tile):
        side = flag(tile // 16 != z_hi)
        own_x, own_y = (tile // 4) % 4 == x, tile % 4 == y

        @pl.when(jnp.logical_not(own_y))
        def _():
            arrived(side, tile, 0)

        @pl.when(jnp.logical_not(own_x))
        def _():
            arrived(side, tile, 1)

        left_rows = [spread(row_tiles, tile, s) for s in range(SLOTS)]
        left_cols = [spread(row_tiles, tile, SLOTS + s) for s in range(SLOTS)]
        right_rows = [spread(col_tiles, tile, s) for s in range(SLOTS)]
        right_cols = [spread(col_tiles, tile, SLOTS + s) for s in range(SLOTS)]
        inner = [[weight(left_cols[a] == right_rows[b]) for b in range(SLOTS)] for a in range(SLOTS)]
        for o in range(KEPT):
            in_row = [weight(left_rows[a] == kept_rows[o].astype(jnp.float32)) for a in range(SLOTS)]
            in_col = [weight(right_cols[b] == kept_cols[o].astype(jnp.float32)) for b in range(SLOTS)]
            for b in range(SLOTS):
                factors = [(in_row[a] * in_col[b] * inner[a][b]).astype(jnp.bfloat16) for a in range(SLOTS)]
                for low in range(0, BLOCK, 16):
                    terms = [factors[a] * row_tiles[tile, pl.ds(a * BLOCK + low, 16), :] for a in range(SLOTS)]
                    chosen[pl.ds(o * BLOCK + low, 16), pl.ds(b * BLOCK, BLOCK)] = terms[0] + terms[1] + terms[2]
        out[...] += jnp.dot(chosen[...], col_tiles[tile, pl.ds(0, META), :], preferred_element_type=jnp.float32)

    def is_early(source, t):
        return (source // 8 == z_hi) | (t > anti_next + 1)

    def multiply_early(t, number):
        place = jnp.maximum((t - MULTIPLY_T) * 3 + number, 0)
        source = k + step * (place // 2 + 1)

        @pl.when((t >= MULTIPLY_T) & is_valid(source) & is_early(source, t))
        def _():
            multiply(source * 2 + place % 2)

    def stream(t, carry):
        source = k + step * t

        def part(other, carry):
            @pl.when(is_valid(source))
            def _():
                goes = goes_on(source)
                tile = source * 2 + other
                for copy in piece_sends(tile, send_row.at[tile], onward):
                    copy.wait_recv()
                    pl.when(goes)(copy.start)
                pair_send(tile).start()

            def between(n, carry):
                multiply_early(t, other + n)
                return carry

            return lax.fori_loop(0, 1 + other, between, carry)

        lax.fori_loop(0, 2, part, 0)

        @pl.when(at_end & (z_hi == 0) & (t == READY_T))
        def _():
            pl.semaphore_wait(ready_anti, anti_count)
            anti_send.start()

            @pl.when(agent)
            def _():
                for distance in range(1, NEAR + 1):
                    across_start(distance)

        @pl.when(agent & (t >= across_low) & (t <= across_high))
        def _():
            across_start(t)

        @pl.when(t == anti_at)
        def _():
            anti_first()

        @pl.when(t == anti_next)
        def _():
            plane_second(1)

        return carry

    lax.fori_loop(1, RUN, stream, 0)

    def rest(n, carry):
        tile = jnp.where(n < 16, z_hi * 16 + n, (1 - z_hi) * 16 + n - 16)
        source, other = tile // 2, tile % 2
        distance = (source - k) * step
        by_pair = (distance < 0) | ((distance == 0) & (other != core))
        done = (distance > 0) & is_early(source, MULTIPLY_T + ((distance - 1) * 2 + other) // 3)

        @pl.when(by_pair)
        def _():
            pair_send(tile).wait_recv()

        @pl.when(jnp.logical_not(done))
        def _():
            multiply(tile)

        return carry

    lax.fori_loop(0, 32, rest, 0)

    def settle(t, carry):
        source = k + step * t

        @pl.when(is_valid(source))
        def _():
            goes = goes_on(source)
            for other in range(2):
                tile = source * 2 + other
                for copy in piece_sends(tile, send_row.at[tile], onward):
                    pl.when(goes)(copy.wait_send)
                pair_send(tile).wait_send()

        return carry

    lax.fori_loop(1, RUN, settle, 0)
    plane_sent(0)
    plane_sent(1)
    pl.when(at_end)(anti_send.wait_send)

    @pl.when(agent)
    def _():
        def across_sent(distance, carry):
            for other in range(2):
                across_send(distance, other).wait_send()
            return carry

        lax.fori_loop(across_low, across_high + 1, across_sent, 0)

        @pl.when(z_hi == 0)
        def _():
            lax.fori_loop(1, NEAR + 1, across_sent, 0)

    pair_send(col).wait_send()
    for wanted, sends in own_sends:

        @pl.when(wanted)
        def _(sends=sends):
            for copy in sends:
                copy.wait_send()


def body(p_blocks, p_rows, p_cols, p_count, kept_rows, kept_cols):
    tiles = 32
    scalars = pl.BlockSpec(memory_space=pltpu.SMEM)
    result = pl.pallas_call(
        square_kernel,
        out_shape=jax.ShapeDtypeStruct((KEPT * BLOCK, BLOCK), jnp.float32),
        in_specs=[scalars] * 5 + [pl.BlockSpec(memory_space=pl.ANY)],
        out_specs=pl.BlockSpec(memory_space=pltpu.VMEM),
        scratch_shapes=[
            pltpu.VMEM((tiles, TILE, BLOCK), jnp.bfloat16),
            pltpu.VMEM((tiles, TILE, BLOCK), jnp.bfloat16),
            pltpu.VMEM((KEPT * BLOCK, META), jnp.bfloat16),
            pltpu.VMEM((16, BLOCK), jnp.bfloat16),
            pltpu.SemaphoreType.DMA((tiles, 3)),
            pltpu.SemaphoreType.DMA((tiles, 2)),
            pltpu.SemaphoreType.DMA,
            pltpu.SemaphoreType.DMA((5,)),
            pltpu.SemaphoreType.DMA((2, 3)),
            pltpu.SemaphoreType.DMA((32,)),
            pltpu.SemaphoreType.DMA((tiles, 3)),
            pltpu.SemaphoreType.DMA((tiles,)),
            pltpu.SemaphoreType.DMA((2, 30)),
            pltpu.SemaphoreType.REGULAR,
            pltpu.SemaphoreType.REGULAR,
        ],
        compiler_params=pltpu.CompilerParams(collective_id=0, has_side_effects=True, vmem_limit_bytes=24 * 2**20),
        name="square_blocks",
    )(
        p_rows.reshape(SLOTS), p_cols.reshape(SLOTS), p_count.reshape(1), kept_rows.reshape(KEPT), kept_cols.reshape(KEPT),
        p_blocks.reshape(META, BLOCK),
    )
    return result.reshape(1, 1, KEPT, BLOCK, BLOCK)


def solution(mesh):
    placed = (
        P("row", "col", None, None, None),
        P("row", "col", None),
        P("row", "col", None),
        P("row", "col"),
        P("row", "col", None),
        P("row", "col", None),
    )
    return jax.shard_map(
        body,
        mesh=mesh,
        in_specs=placed,
        out_specs=P("row", "col", None, None, None),
        check_vma=False,
    )
```

```python
import functools

import jax
import jax.numpy as jnp
from jax import lax
from jax.experimental import pallas as pl
from jax.experimental.pallas import tpu as pltpu
from jax.sharding import PartitionSpec as P

MESH = pl.DeviceIdType.MESH
BLOCK = 128
SLOTS = 3
KEPT = 6
META = SLOTS * BLOCK
TILE = META + 16
HALF = 208
HALVES = ((0, HALF), (HALF, TILE - HALF))
NEAR = 3
RIGHT_FROM = 7
PIECES = ((0, 128), (128, 128), (256, TILE - 256))
RUN = 16
NO_ROW, NO_COL = 20, 30
ANTI_D, READY_T, MULTIPLY_T = 2, 6, 6


def device(z_hi, x, y, k, core):
    return (z_hi * 16 + x * 4 + y, k * 2 + core)


def turn(value, by):
    return lax.rem(value + by, 4)


def flag(condition):
    return jnp.where(condition, 1, 0)


def square_kernel(
    p_rows, p_cols, p_count, kept_rows, kept_cols, blocks, out,
    row_tiles, col_tiles, chosen, meta, row_recv, col_recv, anti_recv, own_sem, send_own, send_anti, send_row, send_pair, send_xy,
    ready_pair, ready_anti,
):
    row, col = lax.axis_index("row"), lax.axis_index("col")
    z_hi, x, y = row // 16, (row // 4) % 4, row % 4
    k, core = col // 2, col % 2
    here = functools.partial(device, z_hi, x, y)
    in_plane = lambda nx, ny: device(z_hi, nx, ny, k, core)
    pair = here(k, 1 - core)
    antipode = device(1 - z_hi, x, y, k, core)

    def signal(semaphore, target):
        pl.semaphore_signal(semaphore, inc=1, device_id=target, device_id_type=MESH)

    first_plane = (z_hi == 0) & (k == 0)
    is_late = first_plane & (x == 0) & (y == 0) & (core == 0)
    late_pair = first_plane & (x == 0) & (y == 0) & (core == 1)
    late_plane = first_plane & (core == 0) & ((x == 0) != (y == 0))

    copies = []

    def local(src, dst, number):
        copy = pltpu.make_async_copy(src, dst, own_sem.at[number])
        copy.start()
        copies.append(copy)

    mine_row, mine_col = row_tiles.at[col], col_tiles.at[row]
    local(blocks, mine_row.at[pl.ds(0, META)], 0)
    local(blocks, mine_col.at[pl.ds(0, META)], 1)

    barrier = pltpu.get_barrier_semaphore()

    @pl.when((core == 0) & (k > 0))
    def _():
        for other in range(2):
            signal(barrier, here(k - 1, other))

    @pl.when((core == 1) & (k < RUN - 1))
    def _():
        for other in range(2):
            signal(barrier, here(k + 1, other))

    @pl.when(jnp.logical_not(is_late))
    def _():
        signal(barrier, pair)
        for d in range(1, 4):
            signal(barrier, in_plane(turn(x, d), y))
            signal(barrier, in_plane(x, turn(y, d)))

    at_end = (k == 0) | (k == RUN - 1)
    agent = ((k == 0) & (core == 1)) | ((k == RUN - 1) & (core == 0))
    across_low = jnp.where(z_hi == 0, 8, 1)
    across_high = jnp.where(z_hi == 0, 14 - NEAR, jnp.where(core == 1, RIGHT_FROM - 1, 15 - RIGHT_FROM))
    anti_count = flag(at_end) + flag(agent) * 2 * (across_high - across_low + 1 + NEAR * (1 - z_hi))
    near_left, near_right = k <= NEAR, k >= RUN - 1 - NEAR
    from_left = jnp.where(z_hi == 0, flag(k < RIGHT_FROM), flag(near_left | ((k >= 8) & jnp.logical_not(near_right)))) == 1
    anti_source = device(
        1 - z_hi, x, y,
        jnp.where(at_end, k, jnp.where(from_left, 0, RUN - 1)), jnp.where(at_end, core, jnp.where(from_left, 1, 0)),
    )
    across = functools.partial(device, 1 - z_hi, x, y)

    @pl.when(z_hi == 0)
    def _():
        signal(barrier, anti_source)

        @pl.when(at_end)
        def _():
            signal(barrier, antipode)

        @pl.when(agent)
        def _():
            for distance in (*range(1, NEAR + 1), *range(8, 15 - NEAR)):
                for other in range(2):
                    signal(barrier, across(jnp.where(core == 1, distance, RUN - 1 - distance), other))

    line = lax.broadcasted_iota(jnp.int32, (16, BLOCK), 0)
    codes = jnp.zeros((16, BLOCK), jnp.int32)
    for slot in range(SLOTS):
        used = slot < p_count[0]
        codes = jnp.where(line == slot, jnp.where(used, p_rows[slot], NO_ROW), codes)
        codes = jnp.where(line == SLOTS + slot, jnp.where(used, p_cols[slot], NO_COL), codes)
    meta[...] = codes.astype(jnp.float32).astype(jnp.bfloat16)
    local(meta, mine_row.at[pl.ds(META, 16)], 2)
    local(meta, mine_col.at[pl.ds(META, 16)], 3)

    expected = (
        flag(k < RUN - 1) + flag(k > 0) + 1 - flag(late_pair) + 6 - flag(late_plane) + z_hi * (1 + anti_count)
    )
    pl.semaphore_wait(barrier, expected)

    @pl.when(z_hi == 1)
    def _():
        signal(ready_anti, anti_source)

    @pl.when(is_late)
    def _():
        signal(ready_pair, pair)
        for d in range(1, 4):
            signal(ready_pair, in_plane(turn(x, d), y))
            signal(ready_pair, in_plane(x, turn(y, d)))

    for copy in copies:
        copy.wait()

    def send(src, dst, send_sem, recv_sem, target):
        return pltpu.make_async_remote_copy(
            src_ref=src, dst_ref=dst, send_sem=send_sem, recv_sem=recv_sem, device_id=target, device_id_type=MESH
        )

    def pair_send(tile):
        return send(row_tiles.at[tile], row_tiles.at[tile], send_pair.at[tile], row_recv.at[tile, 0], pair)

    def piece_sends(tile, send_sem, target):
        parts = [row_tiles.at[tile, pl.ds(low, size)] for low, size in PIECES]
        return [send(part, part, send_sem.at[n], row_recv.at[tile, n], target) for n, part in enumerate(parts)]

    anti_send = send(mine_col, mine_col, own_sem.at[4], anti_recv, antipode)
    own_sends = (
        (k > 0, piece_sends(col, send_own.at[0], here(k - 1, 1))),
        (k < RUN - 1, piece_sends(col, send_own.at[1], here(k + 1, 0))),
    )

    @pl.when((z_hi == 1) & at_end)
    def _():
        anti_send.start()

    for wanted, sends in own_sends:

        @pl.when(wanted)
        def _(sends=sends):
            for copy in sends:
                copy.start()

    def half_send(side, tile, half, number, target):
        low, size = HALVES[half]
        part = col_tiles.at[tile, pl.ds(low, size)]
        return send(part, part, send_xy.at[side, number], col_recv.at[tile, half], target)

    def plane_tile(side, nx, ny):
        z = z_hi if side == 0 else 1 - z_hi
        return z * 16 + nx * 4 + ny

    def plane_own(side):
        mine = plane_tile(side, x, y)
        return [
            half_send(side, mine, half, number * 6 + (d - 1) * 2 + half, in_plane(turn(x, d), y) if along_x else in_plane(x, turn(y, d)))
            for number in range(2)
            for d in (2, 1, 3)
            for half in range(2)
            for along_x in ((half == 0) == (number == 0),)
        ]

    def plane_forward(side, d):
        from_x = plane_tile(side, turn(x, 4 - d), y)
        from_y = plane_tile(side, x, turn(y, 4 - d))
        first = [half_send(side, from_x, 0, 12 + (d - 1) * 6 + e - 1, in_plane(x, turn(y, e))) for e in (2, 1, 3)]
        second = [half_send(side, from_y, 1, 15 + (d - 1) * 6 + e - 1, in_plane(turn(x, e), y)) for e in (2, 1, 3)]
        return first, second

    def arrived(side, tile, half):
        half_send(side, tile, half, 0, pair).wait_recv()

    def plane_first(side):
        for copy in plane_own(side):
            copy.start()

    def plane_second(side):
        for d in (1, 3, 2):
            first, second = plane_forward(side, d)
            arrived(side, plane_tile(side, turn(x, 4 - d), y), 0)
            for copy in first:
                copy.start()
            arrived(side, plane_tile(side, x, turn(y, 4 - d)), 1)
            for copy in second:
                copy.start()

    def plane_sent(side):
        for copy in plane_own(side):
            copy.wait_send()
        for d in range(1, 4):
            for copies_of in plane_forward(side, d):
                for copy in copies_of:
                    copy.wait_send()

    @pl.when(late_plane)
    def _():
        pl.semaphore_wait(ready_pair, 1)

    plane_first(0)

    @pl.when(late_pair)
    def _():
        pl.semaphore_wait(ready_pair, 1)

    pair_send(col).start()
    plane_second(0)

    step = 2 * core - 1
    onward = here(jnp.clip(k - step, 0, RUN - 1), core)

    def is_valid(source):
        return (source >= 0) & (source < RUN)

    def goes_on(source):
        return jnp.where(core == 0, k, RUN - 1 - k) < RUN - 1

    late = RUN - 2
    run0_at = jnp.where(core == 1, jnp.where(k < RIGHT_FROM, 6 + k // 2, late), jnp.minimum(5 + 2 * (RUN - 1 - k), late))
    run1_at = jnp.where(at_end, 8, jnp.where(jnp.where(core == 1, flag(near_left), flag(near_right)) == 1, 10, late))
    anti_at = jnp.where(z_hi == 0, run0_at, run1_at)
    anti_next = jnp.minimum(anti_at + ANTI_D, RUN - 1)

    def across_send(distance, other):
        source = k + step * distance
        tile = source * 2 + other
        target = across(source, other)
        return send(row_tiles.at[tile], col_tiles.at[row], send_anti.at[distance * 2 + other], anti_recv, target)

    def across_start(distance):
        for other in range(2):
            across_send(distance, other).start()

    def anti_first():
        anti_send.wait_recv()
        plane_first(1)

    out[...] = jnp.zeros(out.shape, out.dtype)

    def spread(tiles, tile, number):
        line_of = tiles[tile, pl.ds(META, 16), :].astype(jnp.float32)[number : number + 1, :]
        return jnp.broadcast_to(line_of, (16, BLOCK))

    def weight(condition):
        return jnp.where(condition, 1.0, 0.0).astype(jnp.float32)

    def multiply(tile):
        side = flag(tile // 16 != z_hi)
        own_x, own_y = (tile // 4) % 4 == x, tile % 4 == y

        @pl.when(jnp.logical_not(own_y))
        def _():
            arrived(side, tile, 0)

        @pl.when(jnp.logical_not(own_x))
        def _():
            arrived(side, tile, 1)

        left_rows = [spread(row_tiles, tile, s) for s in range(SLOTS)]
        left_cols = [spread(row_tiles, tile, SLOTS + s) for s in range(SLOTS)]
        right_rows = [spread(col_tiles, tile, s) for s in range(SLOTS)]
        right_cols = [spread(col_tiles, tile, SLOTS + s) for s in range(SLOTS)]
        inner = [[weight(left_cols[a] == right_rows[b]) for b in range(SLOTS)] for a in range(SLOTS)]
        for o in range(KEPT):
            in_row = [weight(left_rows[a] == kept_rows[o].astype(jnp.float32)) for a in range(SLOTS)]
            in_col = [weight(right_cols[b] == kept_cols[o].astype(jnp.float32)) for b in range(SLOTS)]
            for b in range(SLOTS):
                factors = [(in_row[a] * in_col[b] * inner[a][b]).astype(jnp.bfloat16) for a in range(SLOTS)]
                for low in range(0, BLOCK, 16):
                    terms = [factors[a] * row_tiles[tile, pl.ds(a * BLOCK + low, 16), :] for a in range(SLOTS)]
                    chosen[pl.ds(o * BLOCK + low, 16), pl.ds(b * BLOCK, BLOCK)] = terms[0] + terms[1] + terms[2]
        out[...] += jnp.dot(chosen[...], col_tiles[tile, pl.ds(0, META), :], preferred_element_type=jnp.float32)

    def is_early(source, t):
        return (source // 8 == z_hi) | (t > anti_next + 1)

    def multiply_early(t, number):
        place = jnp.maximum((t - MULTIPLY_T) * 3 + number, 0)
        source = k + step * (place // 2 + 1)

        @pl.when((t >= MULTIPLY_T) & is_valid(source) & is_early(source, t))
        def _():
            multiply(source * 2 + place % 2)

    def stream(t, carry):
        source = k + step * t

        def part(other, carry):
            @pl.when(is_valid(source))
            def _():
                goes = goes_on(source)
                tile = source * 2 + other
                for copy in piece_sends(tile, send_row.at[tile], onward):
                    copy.wait_recv()
                    pl.when(goes)(copy.start)
                pair_send(tile).start()

            def between(n, carry):
                multiply_early(t, other + n)
                return carry

            return lax.fori_loop(0, 1 + other, between, carry)

        lax.fori_loop(0, 2, part, 0)

        @pl.when(at_end & (z_hi == 0) & (t == READY_T))
        def _():
            pl.semaphore_wait(ready_anti, anti_count)
            anti_send.start()

            @pl.when(agent)
            def _():
                for distance in range(1, NEAR + 1):
                    across_start(distance)

        @pl.when(agent & (t >= across_low) & (t <= across_high))
        def _():
            across_start(t)

        @pl.when(t == anti_at)
        def _():
            anti_first()

        @pl.when(t == anti_next)
        def _():
            plane_second(1)

        return carry

    lax.fori_loop(1, RUN, stream, 0)

    def rest(n, carry):
        tile = jnp.where(n < 16, z_hi * 16 + n, (1 - z_hi) * 16 + n - 16)
        source, other = tile // 2, tile % 2
        distance = (source - k) * step
        by_pair = (distance < 0) | ((distance == 0) & (other != core))
        done = (distance > 0) & is_early(source, MULTIPLY_T + ((distance - 1) * 2 + other) // 3)

        @pl.when(by_pair)
        def _():
            pair_send(tile).wait_recv()

        @pl.when(jnp.logical_not(done))
        def _():
            multiply(tile)

        return carry

    lax.fori_loop(0, 32, rest, 0)

    def settle(t, carry):
        source = k + step * t

        @pl.when(is_valid(source))
        def _():
            goes = goes_on(source)
            for other in range(2):
                tile = source * 2 + other
                for copy in piece_sends(tile, send_row.at[tile], onward):
                    pl.when(goes)(copy.wait_send)
                pair_send(tile).wait_send()

        return carry

    lax.fori_loop(1, RUN, settle, 0)
    plane_sent(0)
    plane_sent(1)
    pl.when(at_end)(anti_send.wait_send)

    @pl.when(agent)
    def _():
        def across_sent(distance, carry):
            for other in range(2):
                across_send(distance, other).wait_send()
            return carry

        lax.fori_loop(across_low, across_high + 1, across_sent, 0)

        @pl.when(z_hi == 0)
        def _():
            lax.fori_loop(1, NEAR + 1, across_sent, 0)

    pair_send(col).wait_send()
    for wanted, sends in own_sends:

        @pl.when(wanted)
        def _(sends=sends):
            for copy in sends:
                copy.wait_send()


def body(p_blocks, p_rows, p_cols, p_count, kept_rows, kept_cols):
    tiles = 32
    scalars = pl.BlockSpec(memory_space=pltpu.SMEM)
    result = pl.pallas_call(
        square_kernel,
        out_shape=jax.ShapeDtypeStruct((KEPT * BLOCK, BLOCK), jnp.float32),
        in_specs=[scalars] * 5 + [pl.BlockSpec(memory_space=pl.ANY)],
        out_specs=pl.BlockSpec(memory_space=pltpu.VMEM),
        scratch_shapes=[
            pltpu.VMEM((tiles, TILE, BLOCK), jnp.bfloat16),
            pltpu.VMEM((tiles, TILE, BLOCK), jnp.bfloat16),
            pltpu.VMEM((KEPT * BLOCK, META), jnp.bfloat16),
            pltpu.VMEM((16, BLOCK), jnp.bfloat16),
            pltpu.SemaphoreType.DMA((tiles, 3)),
            pltpu.SemaphoreType.DMA((tiles, 2)),
            pltpu.SemaphoreType.DMA,
            pltpu.SemaphoreType.DMA((5,)),
            pltpu.SemaphoreType.DMA((2, 3)),
            pltpu.SemaphoreType.DMA((32,)),
            pltpu.SemaphoreType.DMA((tiles, 3)),
            pltpu.SemaphoreType.DMA((tiles,)),
            pltpu.SemaphoreType.DMA((2, 30)),
            pltpu.SemaphoreType.REGULAR,
            pltpu.SemaphoreType.REGULAR,
        ],
        compiler_params=pltpu.CompilerParams(collective_id=0, has_side_effects=True, vmem_limit_bytes=60 * 2**20),
        name="square_blocks",
    )(
        p_rows.reshape(SLOTS), p_cols.reshape(SLOTS), p_count.reshape(1), kept_rows.reshape(KEPT), kept_cols.reshape(KEPT),
        p_blocks.reshape(META, BLOCK),
    )
    return result.reshape(1, 1, KEPT, BLOCK, BLOCK)


def solution(mesh):
    placed = (
        P("row", "col", None, None, None),
        P("row", "col", None),
        P("row", "col", None),
        P("row", "col"),
        P("row", "col", None),
        P("row", "col", None),
    )
    return jax.shard_map(
        body,
        mesh=mesh,
        in_specs=placed,
        out_specs=P("row", "col", None, None, None),
        check_vma=False,
    )
```
